256 devices in a mesh: ctx: 8 (over y_lo, x), fsdp: 32 (over z, y_hi, core).
Axes of the slice: x: 4, y: 4 (y_hi: 2, y_lo: 2; y = y_hi * 2 + y_lo), z: 8, core: 2. Of those that a mesh axis runs over, the one named last changes fastest.
Arguments:
- signal: bfloat16 [32, 1024, 4096], P('fsdp', 'ctx'), may hold values from -6 to 6
- query: bfloat16 [32, 1024, 4096], P('fsdp', 'ctx'), may hold values from -6 to 6
- grad_out: bfloat16 [32, 1024, 4096], P('fsdp', 'ctx'), may hold values from -6 to 6
- filters: bfloat16 [256, 64], P('fsdp'), may hold values from -0.75 to 0.75
- skip_gain: bfloat16 [4096], P('fsdp'), may hold values from -1 to 1
Outputs:
- grad_query: bfloat16 [32, 1024, 4096], P('fsdp', 'ctx')
- grad_signal: bfloat16 [32, 1024, 4096], P('fsdp', 'ctx')
- grad_filters: float32 [256, 64], P('fsdp')
- grad_skip: float32 [4096], P('fsdp')
The draws below stay inside these ranges and needn't reach their ends.
All inputs are finite; a program needn't handle non-finite values.
Results may differ from the reference program's by a relative error of at most 0.007.
Values may be sent and summed in bfloat16 or wider, within the bound.
A program may use at most 128 MiB of HBM per device.

```python
import jax
import jax.numpy as jnp
from jax import lax

D = 4096
TAPS = 64
GROUPS = 256
SEQS = 32
LEN = 1024
N_CTX = 8
N_FSDP = 32


def strengthened(drawn, key, source, target, blocks, factor):
    def block_of(axis_at):
        return (jnp.arange(drawn.shape[axis_at]) // (drawn.shape[axis_at] // blocks)).reshape((-1,) + (1,) * (drawn.ndim - 1 - axis_at))

    first = jax.random.permutation(key, blocks)[block_of(target)]
    second = (block_of(target) + blocks // 2) % blocks
    return jnp.where((block_of(source) == first) | (block_of(source) == second), factor * drawn, drawn)


def block_levels(own_key, dims, split, least, largest):
    def one(position, shards_of):
        draws = jax.random.uniform(jax.random.fold_in(jax.random.fold_in(own_key, 6), position), (shards_of,), jnp.float32, least / len(split), largest / len(split))
        return jnp.repeat(jnp.exp(draws), dims[position] // shards_of).reshape((-1,) + (1,) * (len(dims) - position - 1))

    factor_of = one(*split[0])
    for cut in split[1:]:
        factor_of = factor_of * one(*cut)
    return factor_of


def centred(rng, dims, scale, bound, pieces=(), kind=jnp.bfloat16):
    result = jax.random.normal(rng, dims, jnp.float32) * scale
    if len(pieces) > 0:
        result = block_levels(rng, dims, pieces, -0.22, 0.18) * result
    return jnp.clip(result, min=-bound, max=bound).astype(kind)


def heavy_noise(key, shape, scale, bound, pieces, heavy, kind=jnp.bfloat16):
    array = scale * jax.random.normal(key, shape, jnp.float32)
    if pieces:
        array = array * block_levels(key, shape, pieces, -0.22, 0.18)
    return jnp.clip(strengthened(array, jax.random.fold_in(key, 3), *heavy), -bound, bound).astype(kind)


def setup_inputs(seed: int = 0) -> dict:
    key_of = jax.random.split(jax.random.key(seed), 6)
    return {
        "signal": centred(key_of[0], (SEQS, LEN, D), 1.0, 6.0, ((0, 32), (1, 8))),
        "query": centred(key_of[1], (SEQS, LEN, D), 1.0, 6.0, ((0, 32), (1, 8))),
        "grad_out": heavy_noise(key_of[2], (SEQS, LEN, D), 1.0, 6.0, ((0, 32), (1, 8)), (0, 2, 32, 2.75)),
        "filters": centred(key_of[3], (GROUPS, TAPS), TAPS ** -0.5, 0.75, ((0, 32),)),
        "skip_gain": jnp.clip(jax.random.uniform(key_of[4], (D,), jnp.float32, -1.0, 1.0) * block_levels(key_of[4], (D,), ((0, 32),), -0.4, 0.0), -1.0, 1.0).astype(jnp.bfloat16),
    }


def toeplitz_pair(filters):
    group_count = filters.shape[0]
    tap_count = filters.shape[1]
    flipped = filters[:, ::-1]
    padded = jnp.concatenate([jnp.zeros((group_count, 1), filters.dtype), flipped, jnp.zeros((group_count, tap_count), filters.dtype)], axis=1)
    tiled = jnp.tile(padded, (1, tap_count))[:, : 2 * tap_count * tap_count]
    return tiled.reshape(group_count, tap_count, 2 * tap_count)


def fold_diagonals(products):
    group_count = products.shape[0]
    tap_count = products.shape[1]
    double = products.shape[2]
    flattened = products.reshape(group_count, tap_count * double)
    flattened = jnp.concatenate([flattened, jnp.zeros((group_count, tap_count), products.dtype)], axis=1)
    skewed = flattened.reshape(group_count, tap_count, double + 1)
    totals = jnp.sum(skewed, axis=1)
    return totals[:, tap_count:0:-1]


def sequence_terms(toeplitz, skip_f, signal_seq, query_seq, grad_seq):
    row_count = signal_seq.shape[0]
    feature_count = signal_seq.shape[1]
    group_count = toeplitz.shape[0]
    tap_count = toeplitz.shape[1]
    group_width = feature_count // group_count
    block_count = row_count // tap_count
    signal_f = signal_seq.astype(jnp.float32)
    extended = jnp.concatenate([jnp.zeros((tap_count, feature_count), jnp.float32), signal_f], axis=0)
    extended = extended.reshape(block_count + 1, tap_count, group_count, group_width)
    paired = jnp.concatenate([extended[:-1], extended[1:]], axis=1)
    filtered = jnp.einsum("gim,nmgc->nigc", toeplitz, paired).reshape(row_count, feature_count)
    mixed = filtered + skip_f * signal_f
    grad_f = grad_seq.astype(jnp.float32)
    grad_query = (grad_f * mixed).astype(jnp.bfloat16)
    gated = (grad_f * query_seq.astype(jnp.float32)).astype(jnp.bfloat16)
    gated_f = lax.optimization_barrier(gated).astype(jnp.float32)
    gated_blocks = gated_f.reshape(block_count, tap_count, group_count, group_width)
    spread = jnp.einsum("gim,nigc->nmgc", toeplitz, gated_blocks)
    later = jnp.concatenate([spread[1:, :tap_count], jnp.zeros((1, tap_count, group_count, group_width), jnp.float32)], axis=0)
    back = (spread[:, tap_count:] + later).reshape(row_count, feature_count)
    grad_signal = (back + skip_f * gated_f).astype(jnp.bfloat16)
    products = jnp.einsum("nigc,nmgc->gim", gated_blocks, paired)
    return grad_query, grad_signal, fold_diagonals(products), jnp.sum(gated_f * signal_f, axis=0)


def reference(signal, query, grad_out, filters, skip_gain):
    toeplitz = toeplitz_pair(filters.astype(jnp.float32))
    skip_f = skip_gain.astype(jnp.float32)

    def one_sequence(totals, inputs):
        grad_query, grad_signal, filter_part, skip_part = sequence_terms(toeplitz, skip_f, inputs[0], inputs[1], inputs[2])
        return (totals[0] + filter_part, totals[1] + skip_part), (grad_query, grad_signal)

    start = (jnp.zeros(filters.shape, jnp.float32), jnp.zeros(skip_gain.shape, jnp.float32))
    totals, outputs = lax.scan(one_sequence, start, (signal, query, grad_out))
    average = 1.0 / (N_CTX * N_FSDP)
    return outputs[0], outputs[1], totals[0] * average, totals[1] * average
```

```python
import functools

import jax
import jax.numpy as jnp
from jax import lax
from jax.experimental import pallas as pl
from jax.experimental.pallas import tpu as pltpu
from jax.sharding import PartitionSpec as P

MESH = pl.DeviceIdType.MESH
BF16 = jnp.bfloat16
F32 = jnp.float32
ROWS = 128
TAPS = 64
LANES = 128
WIDTH = 16
PER_TILE = LANES // WIDTH


def tile_at(j):
    return pl.ds(pl.multiple_of(j * LANES, LANES), LANES)


def lane_index(shape):
    return lax.broadcasted_iota(jnp.int32, shape, len(shape) - 1)


def as_mask(condition):
    return jnp.where(condition, 1.0, 0.0).astype(BF16)


def banded(rows, first):
    bands = []
    for g in range(PER_TILE):
        base = jnp.broadcast_to(rows[g : g + 1], (TAPS, LANES))
        bands.append(pltpu.roll(base, first, 1, stride=1, stride_axis=0).astype(BF16))
    pairs = [jnp.concatenate(bands[p : p + 2], axis=1) for p in range(0, PER_TILE, 2)]
    return jnp.concatenate(pairs, axis=0)


def convolved(bands, window, even, odd):
    parity = []
    for mask in (even, odd):
        kept = window * mask
        parity.append(jnp.concatenate([kept[:ROWS], kept[TAPS : TAPS + ROWS]], axis=1))
    products = jnp.dot(bands, jnp.concatenate(parity, axis=0), preferred_element_type=F32)
    pair_of = lane_index((TAPS, LANES)) // (2 * WIDTH)
    blocks = []
    for n in range(2):
        total = products[:TAPS, n * LANES : (n + 1) * LANES]
        for p in range(1, 4):
            part = products[p * TAPS : (p + 1) * TAPS, n * LANES : (n + 1) * LANES]
            total = jnp.where(pair_of == p, part, total)
        blocks.append(total)
    return jnp.concatenate(blocks, axis=0)


def correlated(later, earlier, masks):
    count = later.shape[0] // WIDTH
    total = None
    for n in range(0, count, 2):
        left, right = [], []
        for k in (n, n + 1):
            block = later[WIDTH * k : WIDTH * (k + 1)]
            left.append(jnp.concatenate([block * mask for mask in masks], axis=0))
            right.append(earlier[WIDTH * k : WIDTH * k + LANES])
        part = lax.dot_general(
            jnp.concatenate(left, axis=1),
            jnp.concatenate(right, axis=1),
            (((1,), (1,)), ((), ())),
            preferred_element_type=F32,
        )
        total = part if total is None else total + part
    return total


def mirror(size):
    i, j = (lax.broadcasted_iota(jnp.int32, (size, size), axis) for axis in (0, 1))
    return as_mask((i // WIDTH == j // WIDTH) & (i % WIDTH + j % WIDTH == WIDTH - 1))


def mirrored(permutation, rows):
    return jnp.dot(permutation, rows, preferred_element_type=F32).astype(BF16)


def folded(products):
    rows = []
    for g in range(PER_TILE):
        block = products[WIDTH * g : WIDTH * (g + 1)]
        skewed = pltpu.roll(block, LANES - WIDTH, 1, stride=1, stride_axis=0)
        rows.append(jnp.sum(skewed, axis=0, keepdims=True))
    return jnp.concatenate(rows, axis=0)


def kernel(
    nf, nc, chunks,
    sig, qry, gout, filt, skip,
    gq_ref, gs_ref, gp_ref,
    s, q, g, gated, flipped, hs, hg, own, skips, packed, fil, rs_src, rs_dst, cx,
    load_sem, hs_send, hs_recv, hg_send, hg_recv, fil_send, fil_recv, rs_send, rs_recv, cx_send, cx_recv,
):
    c = lax.axis_index("ctx")
    me = lax.axis_index("fsdp")
    per_chunk = nf // chunks
    half = chunks // 2
    span = per_chunk * LANES

    barrier = pltpu.get_barrier_semaphore()
    for k in range(1, nc):
        pl.semaphore_signal(barrier, inc=1, device_id={"ctx": lax.rem(c + k, nc)}, device_id_type=MESH)
    for k in range(1, nf):
        pl.semaphore_signal(barrier, inc=1, device_id={"fsdp": lax.rem(me + k, nf)}, device_id_type=MESH)

    loads = [pltpu.make_async_copy(src, dst, load_sem.at[i]) for i, (src, dst) in enumerate(((sig, s), (qry, q), (gout, g)))]
    for load in loads:
        load.start()

    taps = filt[...]
    flip = as_mask(
        lax.broadcasted_iota(jnp.int32, (TAPS, TAPS), 0) + lax.broadcasted_iota(jnp.int32, (TAPS, TAPS), 1) == TAPS - 1
    )
    packed[...] = jnp.zeros_like(packed)
    packed[0:8, 0:TAPS] = taps.astype(F32)
    packed[8:16, 0:TAPS] = jnp.dot(taps, flip, preferred_element_type=F32)
    gain = skip[...].astype(F32)
    packed[0:1, TAPS:LANES] = gain[:, 0:TAPS]
    packed[1:2, TAPS:LANES] = gain[:, TAPS:LANES]
    fil[0] = packed[...].astype(BF16)

    @pl.when(c == 0)
    def _():
        hs[...] = jnp.zeros_like(hs)

    @pl.when(c == nc - 1)
    def _():
        hg[...] = jnp.zeros_like(hg)

    for load in loads:
        load.wait()

    mirror_all, mirror_halo = mirror(ROWS), mirror(TAPS)

    def gate(j, carry):
        at = tile_at(j)
        product = (g[:, at].astype(F32) * q[:, at].astype(F32)).astype(BF16)
        gated[:, at] = product
        flipped[:, at] = mirrored(mirror_all, product)
        skips[j] = jnp.sum(product.astype(F32) * s[:, at].astype(F32), axis=0, keepdims=True)
        return carry

    lax.fori_loop(0, nf, gate, 0)

    def signal_halo(k):
        at = pl.ds(pl.multiple_of(k * span, LANES), span)
        return pltpu.make_async_remote_copy(
            s.at[pl.ds(ROWS - TAPS, TAPS), at], hs.at[:, at], hs_send.at[k], hs_recv.at[k],
            device_id={"ctx": lax.rem(c + 1, nc)}, device_id_type=MESH,
        )

    def gated_halo(k):
        at = pl.ds(pl.multiple_of(k * span, LANES), span)
        return pltpu.make_async_remote_copy(
            gated.at[pl.ds(0, TAPS), at], hg.at[:, at], hg_send.at[k], hg_recv.at[k],
            device_id={"ctx": lax.rem(c + nc - 1, nc)}, device_id_type=MESH,
        )

    pl.semaphore_wait(barrier, nc - 1 + nf - 1)

    for k in range(1, nf):
        pltpu.make_async_remote_copy(
            fil.at[0], fil.at[k], fil_send, fil_recv,
            device_id={"fsdp": lax.rem(me + k, nf)}, device_id_type=MESH,
        ).start()
    for k in range(chunks):
        pl.when(c < nc - 1)(signal_halo(k).start)
        pl.when(c > 0)(gated_halo((k + half) % chunks).start)

    lane_group = lane_index((WIDTH, LANES)) // WIDTH
    masks = [as_mask(lane_group == n) for n in range(PER_TILE)]
    even = as_mask(lane_index((192, LANES)) // WIDTH % 2 == 0)
    odd = as_mask(lane_index((192, LANES)) // WIDTH % 2 == 1)

    def own_part(j, carry):
        at = tile_at(j)
        earlier = jnp.concatenate([jnp.zeros((TAPS, LANES), BF16), s[:, at], jnp.zeros((48, LANES), BF16)], axis=0)
        own[j] = correlated(flipped[:, at], earlier, masks)
        return carry

    lax.fori_loop(0, nf, own_part, 0)

    lane = lane_index((8, LANES))
    row = lax.broadcasted_iota(jnp.int32, (8, LANES), 0)

    def halo_part(j, later, earlier):
        earlier = jnp.concatenate([earlier, jnp.zeros((112, LANES), BF16)], axis=0)
        sums = folded(own[j] + correlated(later, earlier, masks))
        direct = jnp.broadcast_to(skips[j], (8, LANES))
        extra = jnp.where(row == 0, pltpu.roll(direct, TAPS, 1), jnp.where(row == 1, direct, 0.0))
        message = jnp.where(lane < TAPS, sums, extra)
        rs_src[j] = message

        @pl.when(j == me)
        def _():
            rs_dst[0] = message

        @pl.when(j != me)
        def _():
            pltpu.make_async_remote_copy(
                rs_src.at[j], rs_dst.at[lax.rem(j - me + nf, nf)], rs_send, rs_recv,
                device_id={"fsdp": j}, device_id_type=MESH,
            ).start()

    def parameters(j):
        return fil[lax.rem(me - j + nf, nf)].astype(F32)

    def gain_of(params):
        return jnp.where(lane[:1] < TAPS, pltpu.roll(params[0:1], TAPS, 1), params[1:2])

    def query_part(j):
        at = tile_at(j)
        params = parameters(j)
        window = jnp.concatenate([hs[:, at], s[:, at]], axis=0)
        filtered = convolved(banded(params[8:16], 1), window, even, odd)
        mixed = filtered + gain_of(params) * s[:, at].astype(F32)
        gq_ref[:, at] = (g[:, at].astype(F32) * mixed).astype(BF16)

    def signal_part(j):
        at = tile_at(j)
        params = parameters(j)
        window = jnp.concatenate([gated[:, at], hg[:, at]], axis=0)
        forward = jnp.where(lane < TAPS, params[0:8], 0.0)
        back = convolved(banded(forward, 0), window, even, odd)
        gs_ref[:, at] = (back + gain_of(params) * gated[:, at].astype(F32)).astype(BF16)

    def first_half(k, carry):
        pl.when(c > 0)(signal_halo(k).wait_recv)
        pl.when(c < nc - 1)(gated_halo(k + half).wait_recv)
        for i in range(per_chunk):
            j = k * per_chunk + i
            at = tile_at(j)
            halo_part(j, flipped[0:TAPS, at], hs[:, at])
            j = (k + half) * per_chunk + i
            at = tile_at(j)
            halo_part(j, mirrored(mirror_halo, hg[:, at]), s[ROWS - TAPS : ROWS, at])

        @pl.when(k == 0)
        def _():
            pltpu.make_async_copy(fil.at[pl.ds(1, nf - 1)], fil.at[pl.ds(1, nf - 1)], fil_recv).wait()

        for i in range(per_chunk):
            query_part(k * per_chunk + i)
            signal_part((k + half) * per_chunk + i)
        return carry

    lax.fori_loop(0, half, first_half, 0)

    def second_half(k, carry):
        pl.when(c > 0)(signal_halo(k + half).wait_recv)
        pl.when(c < nc - 1)(gated_halo(k).wait_recv)
        for i in range(per_chunk):
            query_part((k + half) * per_chunk + i)
            signal_part(k * per_chunk + i)
        return carry

    lax.fori_loop(0, half, second_half, 0)

    pltpu.make_async_copy(rs_dst.at[pl.ds(1, nf - 1)], rs_dst.at[pl.ds(1, nf - 1)], rs_recv).wait()
    total = rs_dst[0]
    for k in range(1, nf):
        total = total + rs_dst[k]
    cx[0] = total
    for k in range(1, nc):
        pltpu.make_async_remote_copy(
            cx.at[0], cx.at[k], cx_send, cx_recv,
            device_id={"ctx": lax.rem(c + k, nc)}, device_id_type=MESH,
        ).start()
    pltpu.make_async_copy(cx.at[pl.ds(1, nc - 1)], cx.at[pl.ds(1, nc - 1)], cx_recv).wait()
    total = cx[lax.rem(c, nc)]
    for k in range(1, nc):
        total = total + cx[lax.rem(c - k + nc, nc)]
    gp_ref[...] = total * (1.0 / (nc * nf))

    pltpu.make_async_copy(fil.at[pl.ds(1, nf - 1)], fil.at[pl.ds(1, nf - 1)], fil_send).wait()
    pltpu.make_async_copy(rs_src.at[pl.ds(1, nf - 1)], rs_src.at[pl.ds(1, nf - 1)], rs_send).wait()
    pltpu.make_async_copy(cx.at[pl.ds(1, nc - 1)], cx.at[pl.ds(1, nc - 1)], cx_send).wait()
    for k in range(chunks):
        pl.when(c < nc - 1)(signal_halo(k).wait_send)
        pl.when(c > 0)(gated_halo(k).wait_send)


def solution(mesh):
    nc, nf = mesh.shape["ctx"], mesh.shape["fsdp"]
    chunks = min(8, nf)

    def local(signal, query, grad_out, filters, skip_gain):
        features = signal.shape[2]
        whole = (ROWS, features)
        grad_query, grad_signal, params = pl.pallas_call(
            functools.partial(kernel, nf, nc, chunks),
            out_shape=(
                jax.ShapeDtypeStruct(whole, BF16),
                jax.ShapeDtypeStruct(whole, BF16),
                jax.ShapeDtypeStruct((8, LANES), F32),
            ),
            in_specs=[pl.BlockSpec(memory_space=pl.ANY)] * 3 + [pl.BlockSpec(memory_space=pltpu.VMEM)] * 2,
            out_specs=[pl.BlockSpec(memory_space=pltpu.VMEM)] * 3,
            scratch_shapes=[
                pltpu.VMEM(whole, BF16),
                pltpu.VMEM(whole, BF16),
                pltpu.VMEM(whole, BF16),
                pltpu.VMEM(whole, BF16),
                pltpu.VMEM(whole, BF16),
                pltpu.VMEM((TAPS, features), BF16),
                pltpu.VMEM((TAPS, features), BF16),
                pltpu.VMEM((nf, LANES, LANES), F32),
                pltpu.VMEM((nf, 1, LANES), F32),
                pltpu.VMEM((16, LANES), F32),
                pltpu.VMEM((nf, 16, LANES), BF16),
                pltpu.VMEM((nf, 8, LANES), F32),
                pltpu.VMEM((nf, 8, LANES), F32),
                pltpu.VMEM((nc, 8, LANES), F32),
                pltpu.SemaphoreType.DMA((3,)),
                pltpu.SemaphoreType.DMA((chunks,)),
                pltpu.SemaphoreType.DMA((chunks,)),
                pltpu.SemaphoreType.DMA((chunks,)),
                pltpu.SemaphoreType.DMA((chunks,)),
                pltpu.SemaphoreType.DMA,
                pltpu.SemaphoreType.DMA,
                pltpu.SemaphoreType.DMA,
                pltpu.SemaphoreType.DMA,
                pltpu.SemaphoreType.DMA,
                pltpu.SemaphoreType.DMA,
            ],
            compiler_params=pltpu.CompilerParams(
                collective_id=0, has_side_effects=True, vmem_limit_bytes=40 * 1024 * 1024
            ),
        )(signal[0], query[0], grad_out[0], filters, skip_gain.reshape(1, LANES))
        grad_skip = jnp.concatenate([params[0, TAPS:], params[1, TAPS:]])
        return grad_query[None], grad_signal[None], params[:, TAPS - 1 :: -1][:, :TAPS], grad_skip

    return jax.shard_map(
        local,
        mesh=mesh,
        in_specs=(
            P("fsdp", "ctx", None),
            P("fsdp", "ctx", None),
            P("fsdp", "ctx", None),
            P("fsdp", None),
            P("fsdp"),
        ),
        out_specs=(P("fsdp", "ctx", None), P("fsdp", "ctx", None), P("fsdp", None), P("fsdp")),
        check_vma=False,
    )
```

```python
import functools

import jax
import jax.numpy as jnp
from jax import lax
from jax.experimental import pallas as pl
from jax.experimental.pallas import tpu as pltpu
from jax.sharding import PartitionSpec as P

MESH = pl.DeviceIdType.MESH
BF16 = jnp.bfloat16
F32 = jnp.float32
ROWS = 128
TAPS = 64
LANES = 128
WIDTH = 16
PER_TILE = LANES // WIDTH
USED = pl.ds(0, 5)
QUAD = 4
WINDOW = 2


STEP = 4


def packed_rows(taps, gains):
    lane = lane_index((8, LANES))
    row = lax.broadcasted_iota(jnp.int32, (8, LANES), 0)
    beside = pltpu.roll(pltpu.roll(taps, 4, 0), TAPS, 1)
    return jnp.where(row == 4, jnp.broadcast_to(gains, (8, LANES)), jnp.where(lane < TAPS, taps, beside))


def unpacked_taps(rows):
    lane = lane_index((8, LANES))
    row = lax.broadcasted_iota(jnp.int32, (8, LANES), 0)
    beside = pltpu.roll(pltpu.roll(rows, 4, 0), TAPS, 1)
    return jnp.where(lane < TAPS, jnp.where(row < 4, rows, beside), 0.0)


def reversed_taps(taps):
    lane = lane_index((8, LANES))
    return jnp.where(lane < TAPS, jnp.take_along_axis(taps, (LANES + TAPS - 1 - lane) % LANES, axis=1), 0.0)


def in_steps(count, body):
    step = min(STEP, count)

    def run(k, carry):
        for i in range(step):
            body(k * step + i)
        return carry

    lax.fori_loop(0, count // step, run, 0)


def tile_at(j):
    return pl.ds(pl.multiple_of(j * LANES, LANES), LANES)


def lane_index(shape):
    return lax.broadcasted_iota(jnp.int32, shape, len(shape) - 1)


def as_mask(condition):
    return jnp.where(condition, 1.0, 0.0).astype(BF16)


def banded(rows, first):
    bands = []
    for g in range(PER_TILE):
        base = jnp.broadcast_to(rows[g : g + 1], (TAPS, LANES))
        bands.append(pltpu.roll(base, first, 1, stride=1, stride_axis=0).astype(BF16))
    pairs = [jnp.concatenate(bands[p : p + 2], axis=1) for p in range(0, PER_TILE, 2)]
    return jnp.concatenate(pairs, axis=0)


def convolved(bands, window, even, odd):
    parity = []
    for mask in (even, odd):
        kept = window * mask
        parity.append(jnp.concatenate([kept[:ROWS], kept[TAPS : TAPS + ROWS]], axis=1))
    products = jnp.dot(bands, jnp.concatenate(parity, axis=0), preferred_element_type=F32)
    pair_of = lane_index((TAPS, LANES)) // (2 * WIDTH)
    blocks = []
    for n in range(2):
        total = products[:TAPS, n * LANES : (n + 1) * LANES]
        for p in range(1, 4):
            part = products[p * TAPS : (p + 1) * TAPS, n * LANES : (n + 1) * LANES]
            total = jnp.where(pair_of == p, part, total)
        blocks.append(total)
    return jnp.concatenate(blocks, axis=0)


def correlated(blocks, windows, masks):
    total = None
    for n in range(0, TAPS // WIDTH, 2):
        left, right = [], []
        for k in (n, n + 1):
            block = blocks[WIDTH * k : WIDTH * (k + 1)]
            left.append(jnp.concatenate([block * mask for mask in masks], axis=0))
            right.append(windows[WIDTH * k : WIDTH * k + LANES])
        part = lax.dot_general(
            jnp.concatenate(left, axis=1),
            jnp.concatenate(right, axis=1),
            (((1,), (1,)), ((), ())),
            preferred_element_type=F32,
        )
        total = part if total is None else total + part
    return total


def mirror(size):
    i, j = (lax.broadcasted_iota(jnp.int32, (size, size), axis) for axis in (0, 1))
    return as_mask((i // WIDTH == j // WIDTH) & (i % WIDTH + j % WIDTH == WIDTH - 1))


def mirrored(permutation, rows):
    return jnp.dot(permutation, rows, preferred_element_type=F32).astype(BF16)


def folded(products, first):
    rows = []
    for g in range(PER_TILE):
        block = products[WIDTH * g : WIDTH * (g + 1)]
        skewed = pltpu.roll(block, first, 1, stride=1, stride_axis=0)
        rows.append(jnp.sum(skewed, axis=0, keepdims=True))
    return jnp.concatenate(rows, axis=0)


def kernel(
    nf, nc,
    sig, qry, gout, filt_in, skip_in,
    gq_ref, gs_ref, gp_ref,
    filt, skip, s, q, g, gated, flipped, hs, hg, own, skips, fil, rs_src, rs_dst, quad_src, quad_dst, ctx_dst,
    load_sem, hs_send, hs_recv, hg_send, hg_recv, fil_send, fil_recv, sum_send, sum_recv,
):
    c = lax.axis_index("ctx")
    me = lax.axis_index("fsdp")
    nz = nf // QUAD
    own_z, own_u = me // QUAD, lax.rem(me, QUAD)
    half = nz // 2
    span = QUAD * LANES

    def above(k):
        return {"fsdp": lax.rem(own_z + k, nz) * QUAD + own_u}

    def beside(k):
        return {"fsdp": own_z * QUAD + lax.rem(own_u + k, QUAD)}

    def along(k):
        return {"ctx": lax.rem(c + k, nc)}

    following, preceding = {"ctx": lax.rem(c + 1, nc)}, {"ctx": lax.rem(c + nc - 1, nc)}

    def send(src, dst, sends, arrivals, device):
        copy = pltpu.make_async_remote_copy(src, dst, sends, arrivals, device_id=device, device_id_type=MESH)
        copy.start()

    def await_bytes(ref, semaphore):
        pltpu.make_async_copy(ref, ref, semaphore).wait()

    peers = [along(k) for k in range(1, nc)] + [above(k) for k in range(1, nz)] + [beside(k) for k in range(1, QUAD)]
    barrier = pltpu.get_barrier_semaphore()
    for peer in peers:
        pl.semaphore_signal(barrier, inc=1, device_id=peer, device_id_type=MESH)

    loads = [pltpu.make_async_copy(src, dst, load_sem.at[i]) for i, (src, dst) in enumerate(((filt_in, filt), (skip_in, skip), (qry, q), (gout, g), (sig, s)))]
    for load in loads:
        load.start()

    for load in loads[:2]:
        load.wait()
    wide = jnp.concatenate([filt[...].astype(F32), jnp.zeros((8, LANES - TAPS), F32)], axis=1)
    fil[0, 0] = packed_rows(wide, skip[...].astype(F32))

    @pl.when(c == 0)
    def _():
        hs[...] = jnp.zeros_like(hs)

    @pl.when(c == nc - 1)
    def _():
        hg[...] = jnp.zeros_like(hg)

    lane_group = lane_index((WIDTH, LANES)) // WIDTH
    masks = [as_mask(lane_group == n) for n in range(PER_TILE)]
    even = as_mask(lane_index((192, LANES)) // WIDTH % 2 == 0)
    odd = as_mask(lane_index((192, LANES)) // WIDTH % 2 == 1)
    mirror_all = mirror(ROWS)
    nothing = jnp.zeros((48, LANES), BF16)
    middle = half * QUAD

    def gate(j):
        at = tile_at(j)
        gated[:, at] = (g[:, at].astype(F32) * q[:, at].astype(F32)).astype(BF16)

    def own_before(j):
        at = tile_at(j)
        skips[j] = jnp.sum(gated[:, at].astype(F32) * s[:, at].astype(F32), axis=0, keepdims=True)
        turned = mirrored(mirror_all, gated[:, at])
        flipped[:, at] = turned[:TAPS]
        own[j] = correlated(turned[TAPS:], jnp.concatenate([s[:, at], nothing], axis=0), masks)

    def own_after(j):
        at = tile_at(j)
        skips[j] = jnp.sum(gated[:, at].astype(F32) * s[:, at].astype(F32), axis=0, keepdims=True)
        turned = mirrored(mirror_all, s[:, at])
        flipped[:, at] = turned[TAPS:]
        own[j] = correlated(turned[:TAPS], jnp.concatenate([gated[:, at], nothing], axis=0), masks)

    def own_parts():
        in_steps(middle, own_before)
        in_steps(middle, lambda j: own_after(j + middle))

    def gate_all():
        for load in loads[2:4]:
            load.wait()
        in_steps(nf, gate)

    def signal_halo(k):
        at = pl.ds(pl.multiple_of(k * span, LANES), span)
        return pltpu.make_async_remote_copy(
            s.at[pl.ds(ROWS - TAPS, TAPS), at], hs.at[:, at], hs_send.at[k], hs_recv.at[k],
            device_id=following, device_id_type=MESH,
        )

    def gated_halo(k):
        at = pl.ds(pl.multiple_of(k * span, LANES), span)
        return pltpu.make_async_remote_copy(
            gated.at[pl.ds(0, TAPS), at], hg.at[:, at], hg_send.at[k], hg_recv.at[k],
            device_id=preceding, device_id_type=MESH,
        )

    window = min(WINDOW, nz)

    def next_halos(k):
        @pl.when(k < nz - window)
        def _():
            @pl.when(c < nc - 1)
            def _():
                signal_halo(k).wait_send()
                signal_halo(k + window).start()

            @pl.when(c > 0)
            def _():
                gated_halo(lax.rem(k + half, nz)).wait_send()
                gated_halo(lax.rem(k + window + half, nz)).start()

    early = own_z < half
    loads[4].wait()

    @pl.when(early)
    def _():
        gate_all()
        own_parts()

    pl.semaphore_wait(barrier, len(peers))

    quad_filters = fil.at[0, pl.ds(1, QUAD - 1), USED]
    far_filters = fil.at[pl.ds(1, nz - 1), pl.ds(0, QUAD), USED]
    for k in range(1, QUAD):
        send(fil.at[0, 0, USED], fil.at[0, k, USED], fil_send.at[0], fil_recv.at[0], beside(k))
    for k in range(window):
        pl.when(c < nc - 1)(signal_halo(k).start)

    pl.when(jnp.logical_not(early))(gate_all)

    for k in range(window):
        pl.when(c > 0)(gated_halo((k + half) % nz).start)

    await_bytes(quad_filters, fil_recv.at[0])
    for k in range(1, nz):
        send(
            fil.at[0, pl.ds(0, QUAD), USED], fil.at[k, pl.ds(0, QUAD), USED], fil_send.at[1], fil_recv.at[1], above(k)
        )

    pl.when(jnp.logical_not(early))(own_parts)

    def halo_before(j):
        at = tile_at(j)
        windows = jnp.concatenate([hs[:, at], s[0:112, at]], axis=0)
        sums = folded(own[j] + correlated(flipped[:, at], windows, masks), LANES - WIDTH)
        rs_src[j] = packed_rows(reversed_taps(sums), skips[j])

    def halo_after(j):
        at = tile_at(j)
        windows = jnp.concatenate([gated[TAPS:ROWS, at], hg[:, at], nothing], axis=0)
        sums = folded(own[j] + correlated(flipped[:, at], windows, masks), LANES - WIDTH + 1)
        rs_src[j] = packed_rows(sums, skips[j])

    def send_sums(z):
        @pl.when(z != own_z)
        def _():
            send(
                rs_src.at[pl.ds(z * QUAD, QUAD), USED],
                rs_dst.at[lax.rem(z - own_z + nz, nz), pl.ds(0, QUAD), USED],
                sum_send.at[0], sum_recv.at[0], {"fsdp": z * QUAD + own_u},
            )

    def parameters(j):
        return fil[lax.rem(own_z - j // QUAD + nz, nz), lax.rem(own_u - lax.rem(j, QUAD) + QUAD, QUAD)]

    def query_part(j):
        at = tile_at(j)
        params = parameters(j)
        window = jnp.concatenate([hs[:, at], s[:, at]], axis=0)
        filtered = convolved(banded(reversed_taps(unpacked_taps(params)), 1), window, even, odd)
        mixed = filtered + params[4:5] * s[:, at].astype(F32)
        gq_ref[:, at] = (g[:, at].astype(F32) * mixed).astype(BF16)

    def signal_part(j):
        at = tile_at(j)
        params = parameters(j)
        window = jnp.concatenate([gated[:, at], hg[:, at]], axis=0)
        back = convolved(banded(unpacked_taps(params), 0), window, even, odd)
        gs_ref[:, at] = (back + params[4:5] * gated[:, at].astype(F32)).astype(BF16)

    def first_half(k, carry):
        pl.when(c > 0)(signal_halo(k).wait_recv)
        pl.when(c < nc - 1)(gated_halo(k + half).wait_recv)
        next_halos(k)
        for i in range(QUAD):
            halo_before(k * QUAD + i)
            halo_after((k + half) * QUAD + i)
        send_sums(k)
        send_sums(k + half)
        return carry

    lax.fori_loop(0, half, first_half, 0)
    await_bytes(far_filters, fil_recv.at[1])

    far_sums = rs_dst.at[pl.ds(1, nz - 1), pl.ds(0, QUAD), USED]
    quad_sums = quad_dst.at[pl.ds(1, QUAD - 1), USED]
    ctx_sums = ctx_dst.at[pl.ds(1, nc - 1), USED]

    def over_z():
        await_bytes(far_sums, sum_recv.at[0])
        for i in range(QUAD):
            total = rs_src[own_z * QUAD + i, USED]
            for k in range(1, nz):
                total = total + rs_dst[k, i, USED]
            quad_src[i, USED] = total
        for k in range(1, QUAD):
            send(
                quad_src.at[lax.rem(own_u + k, QUAD), USED], quad_dst.at[k, USED],
                sum_send.at[1], sum_recv.at[1], beside(k),
            )

    def over_quad():
        await_bytes(quad_sums, sum_recv.at[1])
        total = quad_src[own_u, USED]
        for k in range(1, QUAD):
            total = total + quad_dst[k, USED]
        ctx_dst[0, USED] = total
        for k in range(1, nc):
            send(ctx_dst.at[0, USED], ctx_dst.at[k, USED], sum_send.at[2], sum_recv.at[2], along(k))

    def over_ctx():
        await_bytes(ctx_sums, sum_recv.at[2])
        total = ctx_dst[c, USED]
        for k in range(1, nc):
            total = total + ctx_dst[lax.rem(c - k + nc, nc), USED]
        gp_ref[...] = jnp.zeros_like(gp_ref)
        gp_ref[USED] = total * (1.0 / (nc * nf))

    def results(k, carry):
        next_halos(k + half)

        @pl.when(k >= half)
        def _():
            pl.when(c > 0)(signal_halo(k).wait_recv)
            pl.when(c < nc - 1)(gated_halo(k - half).wait_recv)

        for i in range(QUAD):
            query_part(k * QUAD + i)
            signal_part(lax.rem(k + half, nz) * QUAD + i)
        pl.when(k == nz - 2)(over_z)
        return carry

    lax.fori_loop(0, nz, results, 0)
    over_quad()
    over_ctx()

    await_bytes(quad_filters, fil_send.at[0])
    await_bytes(far_filters, fil_send.at[1])
    for n, sums in enumerate((far_sums, quad_sums, ctx_sums)):
        await_bytes(sums, sum_send.at[n])
    for k in range(nz - window, nz):
        pl.when(c < nc - 1)(signal_halo(k).wait_send)
        pl.when(c > 0)(gated_halo((k + half) % nz).wait_send)


def hand_over(gq_in, gs_in, params, gq_ref, gs_ref, taps_ref, gain_ref, sems):
    copies = []
    for i, (src, dst) in enumerate(((gq_in, gq_ref), (gs_in, gs_ref))):
        for n in range(2):
            rows = pl.ds(n * TAPS, TAPS)
            copies.append(pltpu.make_async_copy(src.at[rows], dst.at[rows], sems.at[i, n]))
    for copy in copies:
        copy.start()
    whole = params[...]
    taps_ref[...] = unpacked_taps(whole)[:, :TAPS]
    gain_ref[...] = whole[4:5]
    for copy in copies:
        copy.wait()


def solution(mesh):
    nc, nf = mesh.shape["ctx"], mesh.shape["fsdp"]
    nz = nf // QUAD

    def local(signal, query, grad_out, filters, skip_gain):
        features = signal.shape[2]
        whole = (ROWS, features)
        grad_query, grad_signal, params = pl.pallas_call(
            functools.partial(kernel, nf, nc),
            out_shape=(
                jax.ShapeDtypeStruct(whole, BF16),
                jax.ShapeDtypeStruct(whole, BF16),
                jax.ShapeDtypeStruct((8, LANES), F32),
            ),
            in_specs=[pl.BlockSpec(memory_space=pltpu.HBM)] * 5,
            out_specs=[pl.BlockSpec(memory_space=pltpu.VMEM)] * 3,
            scratch_shapes=[
                pltpu.VMEM((8, TAPS), BF16),
                pltpu.VMEM((1, LANES), BF16),
                pltpu.VMEM(whole, BF16),
                pltpu.VMEM(whole, BF16),
                pltpu.VMEM(whole, BF16),
                pltpu.VMEM(whole, BF16),
                pltpu.VMEM((TAPS, features), BF16),
                pltpu.VMEM((TAPS, features), BF16),
                pltpu.VMEM((TAPS, features), BF16),
                pltpu.VMEM((nf, LANES, LANES), F32),
                pltpu.VMEM((nf, 1, LANES), F32),
                pltpu.VMEM((nz, QUAD, 8, LANES), F32),
                pltpu.VMEM((nf, 8, LANES), F32),
                pltpu.VMEM((nz, QUAD, 8, LANES), F32),
                pltpu.VMEM((QUAD, 8, LANES), F32),
                pltpu.VMEM((QUAD, 8, LANES), F32),
                pltpu.VMEM((nc, 8, LANES), F32),
                pltpu.SemaphoreType.DMA((5,)),
                pltpu.SemaphoreType.DMA((nz,)),
                pltpu.SemaphoreType.DMA((nz,)),
                pltpu.SemaphoreType.DMA((nz,)),
                pltpu.SemaphoreType.DMA((nz,)),
                pltpu.SemaphoreType.DMA((2,)),
                pltpu.SemaphoreType.DMA((2,)),
                pltpu.SemaphoreType.DMA((3,)),
                pltpu.SemaphoreType.DMA((3,)),
            ],
            compiler_params=pltpu.CompilerParams(
                collective_id=0, has_side_effects=True, vmem_limit_bytes=40 * 1024 * 1024
            ),
        )(*(pltpu.with_memory_space_constraint(x, pltpu.HBM) for x in (signal[0], query[0], grad_out[0], filters, skip_gain.reshape(1, LANES))))
        grad_query, grad_signal, grad_filters, grad_skip = pl.pallas_call(
            hand_over,
            out_shape=(
                jax.ShapeDtypeStruct(whole, BF16),
                jax.ShapeDtypeStruct(whole, BF16),
                jax.ShapeDtypeStruct((8, TAPS), F32),
                jax.ShapeDtypeStruct((1, LANES), F32),
            ),
            in_specs=[pl.BlockSpec(memory_space=pltpu.VMEM)] * 3,
            out_specs=[pl.BlockSpec(memory_space=pltpu.HBM)] * 2 + [pl.BlockSpec(memory_space=pltpu.VMEM)] * 2,
            scratch_shapes=[pltpu.SemaphoreType.DMA((2, 2))],
        )(*(pltpu.with_memory_space_constraint(x, pltpu.VMEM) for x in (grad_query, grad_signal, params)))
        return grad_query[None], grad_signal[None], grad_filters, grad_skip.reshape(LANES)

    return jax.shard_map(
        local,
        mesh=mesh,
        in_specs=(
            P("fsdp", "ctx", None),
            P("fsdp", "ctx", None),
            P("fsdp", "ctx", None),
            P("fsdp", None),
            P("fsdp"),
        ),
        out_specs=(P("fsdp", "ctx", None), P("fsdp", "ctx", None), P("fsdp", None), P("fsdp")),
        check_vma=False,
    )
```

```python
import functools

import jax
import jax.numpy as jnp
from jax import lax
from jax.experimental import pallas as pl
from jax.experimental.pallas import tpu as pltpu
from jax.sharding import PartitionSpec as P

MESH = pl.DeviceIdType.MESH
BF16 = jnp.bfloat16
F32 = jnp.float32
ROWS = 128
TAPS = 64
LANES = 128
WIDTH = 16
PER_TILE = LANES // WIDTH
USED = pl.ds(0, 5)
QUAD = 4
WINDOW = 3


STEP = 4


def packed_rows(taps, gains):
    lane = lane_index((8, LANES))
    row = lax.broadcasted_iota(jnp.int32, (8, LANES), 0)
    beside = pltpu.roll(pltpu.roll(taps, 4, 0), TAPS, 1)
    return jnp.where(row == 4, jnp.broadcast_to(gains, (8, LANES)), jnp.where(lane < TAPS, taps, beside))


def unpacked_taps(rows):
    lane = lane_index((8, LANES))
    row = lax.broadcasted_iota(jnp.int32, (8, LANES), 0)
    beside = pltpu.roll(pltpu.roll(rows, 4, 0), TAPS, 1)
    return jnp.where(lane < TAPS, jnp.where(row < 4, rows, beside), 0.0)


def reversed_taps(taps):
    lane = lane_index((8, LANES))
    return jnp.where(lane < TAPS, jnp.take_along_axis(taps, (LANES + TAPS - 1 - lane) % LANES, axis=1), 0.0)


def in_steps(count, body):
    step = min(STEP, count)

    def run(k, carry):
        for i in range(step):
            body(k * step + i)
        return carry

    lax.fori_loop(0, count // step, run, 0)


def tile_at(j):
    return pl.ds(pl.multiple_of(j * LANES, LANES), LANES)


def lane_index(shape):
    return lax.broadcasted_iota(jnp.int32, shape, len(shape) - 1)


def as_mask(condition):
    return jnp.where(condition, 1.0, 0.0).astype(BF16)


def banded(rows, first):
    bands = []
    for g in range(PER_TILE):
        base = jnp.broadcast_to(rows[g : g + 1], (TAPS, LANES))
        bands.append(pltpu.roll(base, first, 1, stride=1, stride_axis=0).astype(BF16))
    pairs = [jnp.concatenate(bands[p : p + 2], axis=1) for p in range(0, PER_TILE, 2)]
    return jnp.concatenate(pairs, axis=0)


def convolved(bands, window, even, odd):
    parity = []
    for mask in (even, odd):
        kept = window * mask
        parity.append(jnp.concatenate([kept[:ROWS], kept[TAPS : TAPS + ROWS]], axis=1))
    products = jnp.dot(bands, jnp.concatenate(parity, axis=0), preferred_element_type=F32)
    pair_of = lane_index((TAPS, LANES)) // (2 * WIDTH)
    blocks = []
    for n in range(2):
        total = products[:TAPS, n * LANES : (n + 1) * LANES]
        for p in range(1, 4):
            part = products[p * TAPS : (p + 1) * TAPS, n * LANES : (n + 1) * LANES]
            total = jnp.where(pair_of == p, part, total)
        blocks.append(total)
    return jnp.concatenate(blocks, axis=0)


def correlated(blocks, windows, masks):
    total = None
    for n in range(0, TAPS // WIDTH, 2):
        left, right = [], []
        for k in (n, n + 1):
            block = blocks[WIDTH * k : WIDTH * (k + 1)]
            left.append(jnp.concatenate([block * mask for mask in masks], axis=0))
            right.append(windows[WIDTH * k : WIDTH * k + LANES])
        part = lax.dot_general(
            jnp.concatenate(left, axis=1),
            jnp.concatenate(right, axis=1),
            (((1,), (1,)), ((), ())),
            preferred_element_type=F32,
        )
        total = part if total is None else total + part
    return total


def mirror(size):
    i, j = (lax.broadcasted_iota(jnp.int32, (size, size), axis) for axis in (0, 1))
    return as_mask((i // WIDTH == j // WIDTH) & (i % WIDTH + j % WIDTH == WIDTH - 1))


def mirrored(permutation, rows):
    return jnp.dot(permutation, rows, preferred_element_type=F32).astype(BF16)


def folded(products, first):
    rows = []
    for g in range(PER_TILE):
        block = products[WIDTH * g : WIDTH * (g + 1)]
        skewed = pltpu.roll(block, first, 1, stride=1, stride_axis=0)
        rows.append(jnp.sum(skewed, axis=0, keepdims=True))
    return jnp.concatenate(rows, axis=0)


def kernel(
    nf, nc,
    sig, qry, gout, filt_in, skip_in,
    gq_ref, gs_ref, gp_ref,
    filt, skip, s, q, g, gated, flipped, hs, hg, own, skips, fil, rs_src, rs_dst, quad_src, ctx_dst,
    load_sem, hs_send, hs_recv, hg_send, hg_recv, fil_send, fil_recv, sum_send, sum_recv,
):
    c = lax.axis_index("ctx")
    me = lax.axis_index("fsdp")
    nz = nf // QUAD
    own_z, own_u = me // QUAD, lax.rem(me, QUAD)
    half = nz // 2
    span = QUAD * LANES

    def above(k):
        return {"fsdp": lax.rem(own_z + k, nz) * QUAD + own_u}

    def beside(k):
        return {"fsdp": own_z * QUAD + lax.rem(own_u + k, QUAD)}

    def ring(k, i):
        return {"ctx": lax.rem(c + k, nc), "fsdp": own_z * QUAD + lax.rem(own_u + i, QUAD)}

    def along(k):
        return {"ctx": lax.rem(c + k, nc)}

    following, preceding = {"ctx": lax.rem(c + 1, nc)}, {"ctx": lax.rem(c + nc - 1, nc)}

    def send(src, dst, sends, arrivals, device):
        copy = pltpu.make_async_remote_copy(src, dst, sends, arrivals, device_id=device, device_id_type=MESH)
        copy.start()

    def await_bytes(ref, semaphore):
        pltpu.make_async_copy(ref, ref, semaphore).wait()

    peers = [ring(k, i) for k in range(nc) for i in range(QUAD) if k + i > 0] + [above(k) for k in range(1, nz)]
    barrier = pltpu.get_barrier_semaphore()
    for peer in peers:
        pl.semaphore_signal(barrier, inc=1, device_id=peer, device_id_type=MESH)

    loads = [pltpu.make_async_copy(src, dst, load_sem.at[i]) for i, (src, dst) in enumerate(((filt_in, filt), (skip_in, skip), (qry, q), (gout, g), (sig, s)))]
    for load in loads:
        load.start()

    for load in loads[:2]:
        load.wait()
    wide = jnp.concatenate([filt[...].astype(F32), jnp.zeros((8, LANES - TAPS), F32)], axis=1)
    fil[0, 0] = packed_rows(wide, skip[...].astype(F32))

    @pl.when(c == 0)
    def _():
        hs[...] = jnp.zeros_like(hs)

    @pl.when(c == nc - 1)
    def _():
        hg[...] = jnp.zeros_like(hg)

    lane_group = lane_index((WIDTH, LANES)) // WIDTH
    masks = [as_mask(lane_group == n) for n in range(PER_TILE)]
    even = as_mask(lane_index((192, LANES)) // WIDTH % 2 == 0)
    odd = as_mask(lane_index((192, LANES)) // WIDTH % 2 == 1)
    mirror_all = mirror(ROWS)
    nothing = jnp.zeros((48, LANES), BF16)
    middle = half * QUAD

    def gate(j):
        at = tile_at(j)
        gated[:, at] = (g[:, at].astype(F32) * q[:, at].astype(F32)).astype(BF16)

    def own_before(j):
        at = tile_at(j)
        skips[j] = jnp.sum(gated[:, at].astype(F32) * s[:, at].astype(F32), axis=0, keepdims=True)
        turned = mirrored(mirror_all, gated[:, at])
        flipped[:, at] = turned[:TAPS]
        own[j] = correlated(turned[TAPS:], jnp.concatenate([s[:, at], nothing], axis=0), masks)

    def own_after(j):
        at = tile_at(j)
        skips[j] = jnp.sum(gated[:, at].astype(F32) * s[:, at].astype(F32), axis=0, keepdims=True)
        turned = mirrored(mirror_all, s[:, at])
        flipped[:, at] = turned[TAPS:]
        own[j] = correlated(turned[:TAPS], jnp.concatenate([gated[:, at], nothing], axis=0), masks)

    def own_parts():
        in_steps(middle, own_before)
        in_steps(middle, lambda j: own_after(j + middle))

    def gate_all():
        for load in loads[2:4]:
            load.wait()
        in_steps(nf, gate)

    def signal_halo(k):
        at = pl.ds(pl.multiple_of(k * span, LANES), span)
        return pltpu.make_async_remote_copy(
            s.at[pl.ds(ROWS - TAPS, TAPS), at], hs.at[:, at], hs_send.at[k], hs_recv.at[k],
            device_id=following, device_id_type=MESH,
        )

    def gated_halo(k):
        at = pl.ds(pl.multiple_of(k * span, LANES), span)
        return pltpu.make_async_remote_copy(
            gated.at[pl.ds(0, TAPS), at], hg.at[:, at], hg_send.at[k], hg_recv.at[k],
            device_id=preceding, device_id_type=MESH,
        )

    window = min(WINDOW, nz)

    def next_halos(k):
        @pl.when(k < nz - window)
        def _():
            @pl.when(c < nc - 1)
            def _():
                signal_halo(k).wait_send()
                signal_halo(k + window).start()

            @pl.when(c > 0)
            def _():
                gated_halo(lax.rem(k + half, nz)).wait_send()
                gated_halo(lax.rem(k + window + half, nz)).start()

    early = own_z < half
    loads[4].wait()

    @pl.when(early)
    def _():
        gate_all()
        own_parts()

    pl.semaphore_wait(barrier, len(peers))

    quad_filters = fil.at[0, pl.ds(1, QUAD - 1), USED]
    far_filters = fil.at[pl.ds(1, nz - 1), pl.ds(0, QUAD), USED]
    for k in range(1, QUAD):
        send(fil.at[0, 0, USED], fil.at[0, k, USED], fil_send.at[0], fil_recv.at[0], beside(k))
    for k in range(window):
        pl.when(c < nc - 1)(signal_halo(k).start)

    pl.when(jnp.logical_not(early))(gate_all)

    for k in range(window):
        pl.when(c > 0)(gated_halo((k + half) % nz).start)

    await_bytes(quad_filters, fil_recv.at[0])
    for k in range(1, nz):
        send(
            fil.at[0, pl.ds(0, QUAD), USED], fil.at[k, pl.ds(0, QUAD), USED], fil_send.at[1], fil_recv.at[1], above(k)
        )

    pl.when(jnp.logical_not(early))(own_parts)

    def halo_before(j):
        at = tile_at(j)
        windows = jnp.concatenate([hs[:, at], s[0:112, at]], axis=0)
        sums = folded(own[j] + correlated(flipped[:, at], windows, masks), LANES - WIDTH)
        rs_src[j] = packed_rows(reversed_taps(sums), skips[j])

    def halo_after(j):
        at = tile_at(j)
        windows = jnp.concatenate([gated[TAPS:ROWS, at], hg[:, at], nothing], axis=0)
        sums = folded(own[j] + correlated(flipped[:, at], windows, masks), LANES - WIDTH + 1)
        rs_src[j] = packed_rows(sums, skips[j])

    def send_sums(z):
        @pl.when(z != own_z)
        def _():
            send(
                rs_src.at[pl.ds(z * QUAD, QUAD), USED],
                rs_dst.at[lax.rem(z - own_z + nz, nz), pl.ds(0, QUAD), USED],
                sum_send.at[0], sum_recv.at[0], {"fsdp": z * QUAD + own_u},
            )

    def parameters(j):
        return fil[lax.rem(own_z - j // QUAD + nz, nz), lax.rem(own_u - lax.rem(j, QUAD) + QUAD, QUAD)]

    def query_part(j):
        at = tile_at(j)
        params = parameters(j)
        window = jnp.concatenate([hs[:, at], s[:, at]], axis=0)
        filtered = convolved(banded(reversed_taps(unpacked_taps(params)), 1), window, even, odd)
        mixed = filtered + params[4:5] * s[:, at].astype(F32)
        gq_ref[:, at] = (g[:, at].astype(F32) * mixed).astype(BF16)

    def signal_part(j):
        at = tile_at(j)
        params = parameters(j)
        window = jnp.concatenate([gated[:, at], hg[:, at]], axis=0)
        back = convolved(banded(unpacked_taps(params), 0), window, even, odd)
        gs_ref[:, at] = (back + params[4:5] * gated[:, at].astype(F32)).astype(BF16)

    def first_half(k, carry):
        pl.when(c > 0)(signal_halo(k).wait_recv)
        pl.when(c < nc - 1)(gated_halo(k + half).wait_recv)
        next_halos(k)
        for i in range(QUAD):
            halo_before(k * QUAD + i)
            halo_after((k + half) * QUAD + i)
        send_sums(k)
        send_sums(k + half)
        return carry

    lax.fori_loop(0, half, first_half, 0)
    await_bytes(far_filters, fil_recv.at[1])

    far_sums = rs_dst.at[pl.ds(1, nz - 1), pl.ds(0, QUAD), USED]
    quad_sums = ctx_dst.at[0, pl.ds(1, nc - 1), USED]
    ctx_sums = ctx_dst.at[pl.ds(1, QUAD - 1), pl.ds(0, nc), USED]

    def over_z():
        await_bytes(far_sums, sum_recv.at[0])
        for i in range(QUAD):
            total = rs_src[own_z * QUAD + i, USED]
            for k in range(1, nz):
                total = total + rs_dst[k, i, USED]
            quad_src[i, USED] = total
        for i in range(QUAD):
            owner = lax.rem(own_u + i, QUAD)
            for k in range(nc):
                if k + i > 0:
                    group = min(i, 1)
                    send(
                        quad_src.at[owner, USED], ctx_dst.at[i, k, USED],
                        sum_send.at[1 + group], sum_recv.at[1 + group], ring(k, i),
                    )

    def over_ctx():
        await_bytes(quad_sums, sum_recv.at[1])
        await_bytes(ctx_sums, sum_recv.at[2])
        ctx_dst[0, 0, USED] = quad_src[own_u, USED]
        total = None
        for k in range(nc):
            slot = lax.rem(c - k + nc, nc)
            for i in range(QUAD):
                part = ctx_dst[lax.rem(own_u - i + QUAD, QUAD), slot, USED]
                total = part if total is None else total + part
        gp_ref[...] = jnp.zeros_like(gp_ref)
        gp_ref[USED] = total * (1.0 / (nc * nf))

    def results(k, carry):
        next_halos(k + half)

        @pl.when(k >= half)
        def _():
            pl.when(c > 0)(signal_halo(k).wait_recv)
            pl.when(c < nc - 1)(gated_halo(k - half).wait_recv)

        for i in range(QUAD):
            query_part(k * QUAD + i)
            signal_part(lax.rem(k + half, nz) * QUAD + i)
        pl.when(k == max(nz - 6, 0))(over_z)
        return carry

    lax.fori_loop(0, nz, results, 0)
    over_ctx()

    await_bytes(quad_filters, fil_send.at[0])
    await_bytes(far_filters, fil_send.at[1])
    for n, sums in enumerate((far_sums, quad_sums, ctx_sums)):
        await_bytes(sums, sum_send.at[n])
    for k in range(nz - window, nz):
        pl.when(c < nc - 1)(signal_halo(k).wait_send)
        pl.when(c > 0)(gated_halo((k + half) % nz).wait_send)


def hand_over(gq_in, gs_in, params, gq_ref, gs_ref, taps_ref, gain_ref, sems):
    copies = []
    for i, (src, dst) in enumerate(((gq_in, gq_ref), (gs_in, gs_ref))):
        for n in range(2):
            rows = pl.ds(n * TAPS, TAPS)
            copies.append(pltpu.make_async_copy(src.at[rows], dst.at[rows], sems.at[i, n]))
    for copy in copies:
        copy.start()
    whole = params[...]
    taps_ref[...] = unpacked_taps(whole)[:, :TAPS]
    gain_ref[...] = whole[4:5]
    for copy in copies:
        copy.wait()


def solution(mesh):
    nc, nf = mesh.shape["ctx"], mesh.shape["fsdp"]
    nz = nf // QUAD

    def local(signal, query, grad_out, filters, skip_gain):
        features = signal.shape[2]
        whole = (ROWS, features)
        grad_query, grad_signal, params = pl.pallas_call(
            functools.partial(kernel, nf, nc),
            out_shape=(
                jax.ShapeDtypeStruct(whole, BF16),
                jax.ShapeDtypeStruct(whole, BF16),
                jax.ShapeDtypeStruct((8, LANES), F32),
            ),
            in_specs=[pl.BlockSpec(memory_space=pltpu.HBM)] * 5,
            out_specs=[pl.BlockSpec(memory_space=pltpu.VMEM)] * 3,
            scratch_shapes=[
                pltpu.VMEM((8, TAPS), BF16),
                pltpu.VMEM((1, LANES), BF16),
                pltpu.VMEM(whole, BF16),
                pltpu.VMEM(whole, BF16),
                pltpu.VMEM(whole, BF16),
                pltpu.VMEM(whole, BF16),
                pltpu.VMEM((TAPS, features), BF16),
                pltpu.VMEM((TAPS, features), BF16),
                pltpu.VMEM((TAPS, features), BF16),
                pltpu.VMEM((nf, LANES, LANES), F32),
                pltpu.VMEM((nf, 1, LANES), F32),
                pltpu.VMEM((nz, QUAD, 8, LANES), F32),
                pltpu.VMEM((nf, 8, LANES), F32),
                pltpu.VMEM((nz, QUAD, 8, LANES), F32),
                pltpu.VMEM((QUAD, 8, LANES), F32),
                pltpu.VMEM((QUAD, nc, 8, LANES), F32),
                pltpu.SemaphoreType.DMA((5,)),
                pltpu.SemaphoreType.DMA((nz,)),
                pltpu.SemaphoreType.DMA((nz,)),
                pltpu.SemaphoreType.DMA((nz,)),
                pltpu.SemaphoreType.DMA((nz,)),
                pltpu.SemaphoreType.DMA((2,)),
                pltpu.SemaphoreType.DMA((2,)),
                pltpu.SemaphoreType.DMA((3,)),
                pltpu.SemaphoreType.DMA((3,)),
            ],
            compiler_params=pltpu.CompilerParams(
                collective_id=0, has_side_effects=True, vmem_limit_bytes=40 * 1024 * 1024
            ),
        )(*(pltpu.with_memory_space_constraint(x, pltpu.HBM) for x in (signal[0], query[0], grad_out[0], filters, skip_gain.reshape(1, LANES))))
        grad_query, grad_signal, grad_filters, grad_skip = pl.pallas_call(
            hand_over,
            out_shape=(
                jax.ShapeDtypeStruct(whole, BF16),
                jax.ShapeDtypeStruct(whole, BF16),
                jax.ShapeDtypeStruct((8, TAPS), F32),
                jax.ShapeDtypeStruct((1, LANES), F32),
            ),
            in_specs=[pl.BlockSpec(memory_space=pltpu.VMEM)] * 3,
            out_specs=[pl.BlockSpec(memory_space=pltpu.HBM)] * 2 + [pl.BlockSpec(memory_space=pltpu.VMEM)] * 2,
            scratch_shapes=[pltpu.SemaphoreType.DMA((2, 2))],
        )(*(pltpu.with_memory_space_constraint(x, pltpu.VMEM) for x in (grad_query, grad_signal, params)))
        return grad_query[None], grad_signal[None], grad_filters, grad_skip.reshape(LANES)

    return jax.shard_map(
        local,
        mesh=mesh,
        in_specs=(
            P("fsdp", "ctx", None),
            P("fsdp", "ctx", None),
            P("fsdp", "ctx", None),
            P("fsdp", None),
            P("fsdp"),
        ),
        out_specs=(P("fsdp", "ctx", None), P("fsdp", "ctx", None), P("fsdp", None), P("fsdp")),
        check_vma=False,
    )
```

```python
import functools

import jax
import jax.numpy as jnp
from jax import lax
from jax.experimental import pallas as pl
from jax.experimental.pallas import tpu as pltpu
from jax.sharding import PartitionSpec as P

MESH = pl.DeviceIdType.MESH
BF16 = jnp.bfloat16
F32 = jnp.float32
ROWS = 128
TAPS = 64
LANES = 128
WIDTH = 16
PER_TILE = LANES // WIDTH
USED = pl.ds(0, 5)
QUAD = 4
WINDOW = 3


STEP = 8


def packed_rows(taps, gains):
    lane = lane_index((8, LANES))
    row = lax.broadcasted_iota(jnp.int32, (8, LANES), 0)
    beside = pltpu.roll(pltpu.roll(taps, 4, 0), TAPS, 1)
    return jnp.where(row == 4, jnp.broadcast_to(gains, (8, LANES)), jnp.where(lane < TAPS, taps, beside))


def unpacked_taps(rows):
    lane = lane_index((8, LANES))
    row = lax.broadcasted_iota(jnp.int32, (8, LANES), 0)
    beside = pltpu.roll(pltpu.roll(rows, 4, 0), TAPS, 1)
    return jnp.where(lane < TAPS, jnp.where(row < 4, rows, beside), 0.0)


def reversed_taps(taps):
    lane = lane_index((8, LANES))
    return jnp.where(lane < TAPS, jnp.take_along_axis(taps, (LANES + TAPS - 1 - lane) % LANES, axis=1), 0.0)


def in_steps(count, body):
    step = min(STEP, count)

    def run(k, carry):
        for i in range(step):
            body(k * step + i)
        return carry

    lax.fori_loop(0, count // step, run, 0)


def tile_at(j):
    return pl.ds(pl.multiple_of(j * LANES, LANES), LANES)


def lane_index(shape):
    return lax.broadcasted_iota(jnp.int32, shape, len(shape) - 1)


def as_mask(condition):
    return jnp.where(condition, 1.0, 0.0).astype(BF16)


def banded(rows, first):
    bands = []
    for g in range(PER_TILE):
        base = jnp.broadcast_to(rows[g : g + 1], (TAPS, LANES))
        bands.append(pltpu.roll(base, first, 1, stride=1, stride_axis=0).astype(BF16))
    pairs = [jnp.concatenate(bands[p : p + 2], axis=1) for p in range(0, PER_TILE, 2)]
    return jnp.concatenate(pairs, axis=0)


def convolved(bands, window, even, odd):
    parity = []
    for mask in (even, odd):
        kept = window * mask
        parity.append(jnp.concatenate([kept[:ROWS], kept[TAPS : TAPS + ROWS]], axis=1))
    products = jnp.dot(bands, jnp.concatenate(parity, axis=0), preferred_element_type=F32)
    pair_of = lane_index((TAPS, LANES)) // (2 * WIDTH)
    blocks = []
    for n in range(2):
        total = products[:TAPS, n * LANES : (n + 1) * LANES]
        for p in range(1, 4):
            part = products[p * TAPS : (p + 1) * TAPS, n * LANES : (n + 1) * LANES]
            total = jnp.where(pair_of == p, part, total)
        blocks.append(total)
    return jnp.concatenate(blocks, axis=0)


def correlated(blocks, windows, masks):
    total = None
    for n in range(0, TAPS // WIDTH, 2):
        left, right = [], []
        for k in (n, n + 1):
            block = blocks[WIDTH * k : WIDTH * (k + 1)]
            left.append(jnp.concatenate([block * mask for mask in masks], axis=0))
            right.append(windows[WIDTH * k : WIDTH * k + LANES])
        part = lax.dot_general(
            jnp.concatenate(left, axis=1),
            jnp.concatenate(right, axis=1),
            (((1,), (1,)), ((), ())),
            preferred_element_type=F32,
        )
        total = part if total is None else total + part
    return total


def mirror(size):
    i, j = (lax.broadcasted_iota(jnp.int32, (size, size), axis) for axis in (0, 1))
    return as_mask((i // WIDTH == j // WIDTH) & (i % WIDTH + j % WIDTH == WIDTH - 1))


def mirrored(permutation, rows):
    return jnp.dot(permutation, rows, preferred_element_type=F32).astype(BF16)


def folded(products, first):
    rows = []
    for g in range(PER_TILE):
        block = products[WIDTH * g : WIDTH * (g + 1)]
        skewed = pltpu.roll(block, first, 1, stride=1, stride_axis=0)
        rows.append(jnp.sum(skewed, axis=0, keepdims=True))
    return jnp.concatenate(rows, axis=0)


def kernel(
    nf, nc,
    sig, qry, gout, filt_in, skip_in,
    gq_ref, gs_ref, gp_ref,
    filt, skip, s, q, g, gated, flipped, hs, hg, own, skips, fil, rs_src, rs_dst, quad_src, ctx_dst,
    load_sem, hs_send, hs_recv, hg_send, hg_recv, fil_send, fil_recv, sum_send, sum_recv,
):
    c = lax.axis_index("ctx")
    me = lax.axis_index("fsdp")
    nz = nf // QUAD
    own_z, own_u = me // QUAD, lax.rem(me, QUAD)
    half = nz // 2
    span = QUAD * LANES

    def above(k):
        return {"fsdp": lax.rem(own_z + k, nz) * QUAD + own_u}

    def beside(k):
        return {"fsdp": own_z * QUAD + lax.rem(own_u + k, QUAD)}

    def ring(k, i):
        return {"ctx": lax.rem(c + k, nc), "fsdp": own_z * QUAD + lax.rem(own_u + i, QUAD)}

    def along(k):
        return {"ctx": lax.rem(c + k, nc)}

    following, preceding = {"ctx": lax.rem(c + 1, nc)}, {"ctx": lax.rem(c + nc - 1, nc)}

    def send(src, dst, sends, arrivals, device):
        copy = pltpu.make_async_remote_copy(src, dst, sends, arrivals, device_id=device, device_id_type=MESH)
        copy.start()

    def await_bytes(ref, semaphore):
        pltpu.make_async_copy(ref, ref, semaphore).wait()

    peers = [ring(k, i) for k in range(nc) for i in range(QUAD) if k + i > 0] + [above(k) for k in range(1, nz)]
    barrier = pltpu.get_barrier_semaphore()
    for peer in peers:
        pl.semaphore_signal(barrier, inc=1, device_id=peer, device_id_type=MESH)

    loads = [pltpu.make_async_copy(src, dst, load_sem.at[i]) for i, (src, dst) in enumerate(((filt_in, filt), (skip_in, skip), (qry, q), (gout, g), (sig, s)))]
    for load in loads:
        load.start()

    for load in loads[:2]:
        load.wait()
    wide = jnp.concatenate([filt[...].astype(F32), jnp.zeros((8, LANES - TAPS), F32)], axis=1)
    fil[0, 0] = packed_rows(wide, skip[...].astype(F32))

    @pl.when(c == 0)
    def _():
        hs[...] = jnp.zeros_like(hs)

    @pl.when(c == nc - 1)
    def _():
        hg[...] = jnp.zeros_like(hg)

    lane_group = lane_index((WIDTH, LANES)) // WIDTH
    masks = [as_mask(lane_group == n) for n in range(PER_TILE)]
    even = as_mask(lane_index((192, LANES)) // WIDTH % 2 == 0)
    odd = as_mask(lane_index((192, LANES)) // WIDTH % 2 == 1)
    mirror_all = mirror(ROWS)
    nothing = jnp.zeros((48, LANES), BF16)
    middle = half * QUAD

    def gate(j):
        at = tile_at(j)
        gated[:, at] = (g[:, at].astype(F32) * q[:, at].astype(F32)).astype(BF16)

    def own_before(j):
        at = tile_at(j)
        skips[j] = jnp.sum(gated[:, at].astype(F32) * s[:, at].astype(F32), axis=0, keepdims=True)
        turned = mirrored(mirror_all, gated[:, at])
        flipped[:, at] = turned[:TAPS]
        own[j] = correlated(turned[TAPS:], jnp.concatenate([s[:, at], nothing], axis=0), masks)

    def own_after(j):
        at = tile_at(j)
        skips[j] = jnp.sum(gated[:, at].astype(F32) * s[:, at].astype(F32), axis=0, keepdims=True)
        turned = mirrored(mirror_all, s[:, at])
        flipped[:, at] = turned[TAPS:]
        own[j] = correlated(turned[:TAPS], jnp.concatenate([gated[:, at], nothing], axis=0), masks)

    def own_parts():
        in_steps(middle, own_before)
        in_steps(middle, lambda j: own_after(j + middle))

    def gate_all():
        for load in loads[2:4]:
            load.wait()
        in_steps(nf, gate)

    def signal_halo(k):
        at = pl.ds(pl.multiple_of(k * span, LANES), span)
        return pltpu.make_async_remote_copy(
            s.at[pl.ds(ROWS - TAPS, TAPS), at], hs.at[:, at], hs_send.at[k], hs_recv.at[k],
            device_id=following, device_id_type=MESH,
        )

    def gated_halo(k):
        at = pl.ds(pl.multiple_of(k * span, LANES), span)
        return pltpu.make_async_remote_copy(
            gated.at[pl.ds(0, TAPS), at], hg.at[:, at], hg_send.at[k], hg_recv.at[k],
            device_id=preceding, device_id_type=MESH,
        )

    window = min(WINDOW, nz)

    def next_halos(k):
        @pl.when(k < nz - window)
        def _():
            @pl.when(c < nc - 1)
            def _():
                signal_halo(k).wait_send()
                signal_halo(k + window).start()

            @pl.when(c > 0)
            def _():
                gated_halo(lax.rem(k + half, nz)).wait_send()
                gated_halo(lax.rem(k + window + half, nz)).start()

    early = own_z < half
    loads[4].wait()

    @pl.when(early)
    def _():
        gate_all()
        own_parts()

    pl.semaphore_wait(barrier, len(peers))

    quad_filters = fil.at[0, pl.ds(1, QUAD - 1), USED]
    far_filters = fil.at[pl.ds(1, nz - 1), pl.ds(0, QUAD), USED]
    for k in range(1, QUAD):
        send(fil.at[0, 0, USED], fil.at[0, k, USED], fil_send.at[0], fil_recv.at[0], beside(k))
    for k in range(window):
        pl.when(c < nc - 1)(signal_halo(k).start)

    pl.when(jnp.logical_not(early))(gate_all)

    for k in range(window):
        pl.when(c > 0)(gated_halo((k + half) % nz).start)

    await_bytes(quad_filters, fil_recv.at[0])
    for k in range(1, nz):
        send(
            fil.at[0, pl.ds(0, QUAD), USED], fil.at[k, pl.ds(0, QUAD), USED], fil_send.at[1], fil_recv.at[1], above(k)
        )

    pl.when(jnp.logical_not(early))(own_parts)

    def halo_before(j):
        at = tile_at(j)
        windows = jnp.concatenate([hs[:, at], s[0:112, at]], axis=0)
        sums = folded(own[j] + correlated(flipped[:, at], windows, masks), LANES - WIDTH)
        rs_src[j] = packed_rows(reversed_taps(sums), skips[j])

    def halo_after(j):
        at = tile_at(j)
        windows = jnp.concatenate([gated[TAPS:ROWS, at], hg[:, at], nothing], axis=0)
        sums = folded(own[j] + correlated(flipped[:, at], windows, masks), LANES - WIDTH + 1)
        rs_src[j] = packed_rows(sums, skips[j])

    def send_sums(z):
        @pl.when(z != own_z)
        def _():
            send(
                rs_src.at[pl.ds(z * QUAD, QUAD), USED],
                rs_dst.at[lax.rem(z - own_z + nz, nz), pl.ds(0, QUAD), USED],
                sum_send.at[0], sum_recv.at[0], {"fsdp": z * QUAD + own_u},
            )

    def parameters(j):
        return fil[lax.rem(own_z - j // QUAD + nz, nz), lax.rem(own_u - lax.rem(j, QUAD) + QUAD, QUAD)]

    def query_part(j):
        at = tile_at(j)
        params = parameters(j)
        window = jnp.concatenate([hs[:, at], s[:, at]], axis=0)
        filtered = convolved(banded(reversed_taps(unpacked_taps(params)), 1), window, even, odd)
        mixed = filtered + params[4:5] * s[:, at].astype(F32)
        gq_ref[:, at] = (g[:, at].astype(F32) * mixed).astype(BF16)

    def signal_part(j):
        at = tile_at(j)
        params = parameters(j)
        window = jnp.concatenate([gated[:, at], hg[:, at]], axis=0)
        back = convolved(banded(unpacked_taps(params), 0), window, even, odd)
        gs_ref[:, at] = (back + params[4:5] * gated[:, at].astype(F32)).astype(BF16)

    def first_half(k, carry):
        pl.when(c > 0)(signal_halo(k).wait_recv)
        pl.when(c < nc - 1)(gated_halo(k + half).wait_recv)
        next_halos(k)
        for i in range(QUAD):
            halo_before(k * QUAD + i)
            halo_after((k + half) * QUAD + i)
        send_sums(k)
        send_sums(k + half)
        return carry

    lax.fori_loop(0, half, first_half, 0)
    await_bytes(far_filters, fil_recv.at[1])

    far_sums = rs_dst.at[pl.ds(1, nz - 1), pl.ds(0, QUAD), USED]
    quad_sums = ctx_dst.at[0, pl.ds(1, nc - 1), USED]
    ctx_sums = ctx_dst.at[pl.ds(1, QUAD - 1), pl.ds(0, nc), USED]

    def over_z():
        await_bytes(far_sums, sum_recv.at[0])
        for i in range(QUAD):
            total = rs_src[own_z * QUAD + i, USED]
            for k in range(1, nz):
                total = total + rs_dst[k, i, USED]
            quad_src[i, USED] = total
        for i in range(QUAD):
            owner = lax.rem(own_u + i, QUAD)
            for k in range(nc):
                if k + i > 0:
                    group = min(i, 1)
                    send(
                        quad_src.at[owner, USED], ctx_dst.at[i, k, USED],
                        sum_send.at[1 + group], sum_recv.at[1 + group], ring(k, i),
                    )

    def over_ctx():
        await_bytes(quad_sums, sum_recv.at[1])
        await_bytes(ctx_sums, sum_recv.at[2])
        ctx_dst[0, 0, USED] = quad_src[own_u, USED]
        total = None
        for k in range(nc):
            slot = lax.rem(c - k + nc, nc)
            for i in range(QUAD):
                part = ctx_dst[lax.rem(own_u - i + QUAD, QUAD), slot, USED]
                total = part if total is None else total + part
        gp_ref[...] = jnp.zeros_like(gp_ref)
        gp_ref[USED] = total * (1.0 / (nc * nf))

    def results(k, carry):
        next_halos(k + half)

        @pl.when(k >= half)
        def _():
            pl.when(c > 0)(signal_halo(k).wait_recv)
            pl.when(c < nc - 1)(gated_halo(k - half).wait_recv)

        for i in range(QUAD):
            query_part(k * QUAD + i)
            signal_part(lax.rem(k + half, nz) * QUAD + i)
        pl.when(k == max(nz - 6, 0))(over_z)
        return carry

    lax.fori_loop(0, nz, results, 0)
    over_ctx()

    await_bytes(quad_filters, fil_send.at[0])
    await_bytes(far_filters, fil_send.at[1])
    for n, sums in enumerate((far_sums, quad_sums, ctx_sums)):
        await_bytes(sums, sum_send.at[n])
    for k in range(nz - window, nz):
        pl.when(c < nc - 1)(signal_halo(k).wait_send)
        pl.when(c > 0)(gated_halo((k + half) % nz).wait_send)


def hand_over(gq_in, gs_in, params, gq_ref, gs_ref, taps_ref, gain_ref, sems):
    copies = []
    for i, (src, dst) in enumerate(((gq_in, gq_ref), (gs_in, gs_ref))):
        for n in range(2):
            rows = pl.ds(n * TAPS, TAPS)
            copies.append(pltpu.make_async_copy(src.at[rows], dst.at[rows], sems.at[i, n]))
    for copy in copies:
        copy.start()
    whole = params[...]
    taps_ref[...] = unpacked_taps(whole)[:, :TAPS]
    gain_ref[...] = whole[4:5]
    for copy in copies:
        copy.wait()


def solution(mesh):
    nc, nf = mesh.shape["ctx"], mesh.shape["fsdp"]
    nz = nf // QUAD

    def local(signal, query, grad_out, filters, skip_gain):
        features = signal.shape[2]
        whole = (ROWS, features)
        grad_query, grad_signal, params = pl.pallas_call(
            functools.partial(kernel, nf, nc),
            out_shape=(
                jax.ShapeDtypeStruct(whole, BF16),
                jax.ShapeDtypeStruct(whole, BF16),
                jax.ShapeDtypeStruct((8, LANES), F32),
            ),
            in_specs=[pl.BlockSpec(memory_space=pltpu.HBM)] * 5,
            out_specs=[pl.BlockSpec(memory_space=pltpu.VMEM)] * 3,
            scratch_shapes=[
                pltpu.VMEM((8, TAPS), BF16),
                pltpu.VMEM((1, LANES), BF16),
                pltpu.VMEM(whole, BF16),
                pltpu.VMEM(whole, BF16),
                pltpu.VMEM(whole, BF16),
                pltpu.VMEM(whole, BF16),
                pltpu.VMEM((TAPS, features), BF16),
                pltpu.VMEM((TAPS, features), BF16),
                pltpu.VMEM((TAPS, features), BF16),
                pltpu.VMEM((nf, LANES, LANES), F32),
                pltpu.VMEM((nf, 1, LANES), F32),
                pltpu.VMEM((nz, QUAD, 8, LANES), F32),
                pltpu.VMEM((nf, 8, LANES), F32),
                pltpu.VMEM((nz, QUAD, 8, LANES), F32),
                pltpu.VMEM((QUAD, 8, LANES), F32),
                pltpu.VMEM((QUAD, nc, 8, LANES), F32),
                pltpu.SemaphoreType.DMA((5,)),
                pltpu.SemaphoreType.DMA((nz,)),
                pltpu.SemaphoreType.DMA((nz,)),
                pltpu.SemaphoreType.DMA((nz,)),
                pltpu.SemaphoreType.DMA((nz,)),
                pltpu.SemaphoreType.DMA((2,)),
                pltpu.SemaphoreType.DMA((2,)),
                pltpu.SemaphoreType.DMA((3,)),
                pltpu.SemaphoreType.DMA((3,)),
            ],
            compiler_params=pltpu.CompilerParams(
                collective_id=0, has_side_effects=True, vmem_limit_bytes=40 * 1024 * 1024
            ),
        )(*(pltpu.with_memory_space_constraint(x, pltpu.HBM) for x in (signal[0], query[0], grad_out[0], filters, skip_gain.reshape(1, LANES))))
        grad_query, grad_signal, grad_filters, grad_skip = pl.pallas_call(
            hand_over,
            out_shape=(
                jax.ShapeDtypeStruct(whole, BF16),
                jax.ShapeDtypeStruct(whole, BF16),
                jax.ShapeDtypeStruct((8, TAPS), F32),
                jax.ShapeDtypeStruct((1, LANES), F32),
            ),
            in_specs=[pl.BlockSpec(memory_space=pltpu.VMEM)] * 3,
            out_specs=[pl.BlockSpec(memory_space=pltpu.HBM)] * 2 + [pl.BlockSpec(memory_space=pltpu.VMEM)] * 2,
            scratch_shapes=[pltpu.SemaphoreType.DMA((2, 2))],
        )(*(pltpu.with_memory_space_constraint(x, pltpu.VMEM) for x in (grad_query, grad_signal, params)))
        return grad_query[None], grad_signal[None], grad_filters, grad_skip.reshape(LANES)

    return jax.shard_map(
        local,
        mesh=mesh,
        in_specs=(
            P("fsdp", "ctx", None),
            P("fsdp", "ctx", None),
            P("fsdp", "ctx", None),
            P("fsdp", None),
            P("fsdp"),
        ),
        out_specs=(P("fsdp", "ctx", None), P("fsdp", "ctx", None), P("fsdp", None), P("fsdp")),
        check_vma=False,
    )
```
